32 devices in a mesh: mem: 4 (over x, core), tile: 8 (over z, y).
Axes of the slice: x: 2, y: 2, z: 4, core: 2. Of those that a mesh axis runs over, the one named last changes fastest.
Arguments:
- control: float32 [8, 32, 320, 160], P('mem', None, 'tile'), may hold values from -6 to 6
- ens_perts: float32 [8, 2, 32, 320, 160], P('mem', None, None, 'tile'), may hold values from -8 to 8
- vert_corr: float32 [32, 32], replicated, may hold values from -1 to 1
- slab_wts: float32 [8, 4], replicated, may hold values from 0.25 to 2
- level_slab: int32 [32], replicated, may hold values from 0 to 7, as said below
Outputs:
- wind_share: float32 [2, 32, 320, 160], P(None, 'mem', 'tile')
- gradient: float32 [8, 32, 320, 160], P('mem', None, 'tile')
The draws below stay inside these ranges and needn't reach their ends.
Inputs may be any that keep to these rules, and one draw needn't show every extreme that they name: `level_slab`: each slab holds a contiguous run of levels and slab numbers never fall with the level; every slab holds 1 to 8 levels, and one slab holds exactly 8.
All inputs are finite; a program needn't handle non-finite values.
Results may differ from the reference program's by a relative error of at most 0.0001.
Values sent between devices are 32-bit elements; how exact they have to be, the bound alone decides.
A program may use at most 128 MiB of HBM per device.

```python
import math
import jax
import jax.numpy as jnp
from jax import lax

NX = 320
NY = 160
COMP = 2
L = 32
M = 8
SLABS = 8
CAP = 8


def draw_level_slab(key, part):
    key_pick, key_perm = jax.random.split(jax.random.fold_in(key, 17))
    full_slab = jax.random.randint(key_pick, (), 0, SLABS)
    extra = L - CAP - (SLABS - 1)
    candidates = (SLABS - 1) * (CAP - 1)
    order = jax.random.permutation(key_perm, candidates)
    chosen = (order < extra).astype(jnp.int32)
    owners = jnp.arange(candidates) // (CAP - 1)
    others = jnp.arange(SLABS - 1)
    extra_counts = jnp.sum((owners[None, :] == others[:, None]).astype(jnp.int32) * chosen[None, :], axis=1)
    actual = others + (others >= full_slab).astype(others.dtype)
    counts = jnp.zeros((SLABS,), jnp.int32).at[actual].set((1 + extra_counts).astype(jnp.int32))
    counts = counts.at[full_slab].set(CAP)
    ends = jnp.cumsum(counts)
    levels = jnp.arange(L)
    return jnp.sum((ends[None, :] <= levels[:, None]).astype(jnp.int32), axis=1).astype(jnp.int32)


def raised(result, own_key, source, target, blocks, factor):
    def block_of(dim):
        return (jnp.arange(result.shape[dim]) // (result.shape[dim] // blocks)).reshape((-1,) + (1,) * (result.ndim - 1 - dim))

    one_side = jax.random.permutation(own_key, blocks)[block_of(target)]
    second = (block_of(target) + blocks // 2) % blocks
    return jnp.where((block_of(source) == one_side) | (block_of(source) == second), factor * result, result)


def steps_of(rng, shape, cuts, low, top_value):
    def one(axis_at, shards_of):
        steps = jax.random.uniform(jax.random.fold_in(jax.random.fold_in(rng, 6), axis_at), (shards_of,), jnp.float32, low / len(cuts), top_value / len(cuts))
        return jnp.repeat(jnp.exp(steps), shape[axis_at] // shards_of).reshape((-1,) + (1,) * (len(shape) - axis_at - 1))

    level = one(*cuts[0])
    for cut in cuts[1:]:
        level = level * one(*cut)
    return level


def bell_draw(stream_key, extent, width, bound, shards=(), kind=jnp.bfloat16):
    loudness = steps_of(stream_key, extent, shards, -0.22, 0.18) if shards else 1.0
    result = jax.random.normal(stream_key, extent, jnp.float32) * width * loudness
    return jnp.minimum(jnp.maximum(result, -bound), bound).astype(kind)


def gaussian_with(rng, extent, deviation, reach, cuts, heavy, kind=jnp.bfloat16):
    drawn = deviation * jax.random.normal(rng, extent, jnp.float32)
    if cuts:
        drawn = drawn * steps_of(rng, extent, cuts, -0.22, 0.18)
    return jnp.clip(raised(drawn, jax.random.fold_in(rng, 3), *heavy), -reach, reach).astype(kind)


def setup_inputs(seed: int = 0) -> dict:
    key_list = jax.random.split(jax.random.key(seed), 6)
    return {
        "control": bell_draw(key_list[0], (M, L, NX, NY), 1.0, 6.0, ((0, 4), (2, 8)), jnp.float32),
        "ens_perts": gaussian_with(key_list[1], (M, COMP, L, NX, NY), 1.0, 8.0, ((0, 4), (3, 8)), (0, 2, 4, 2.0), jnp.float32),
        "vert_corr": bell_draw(key_list[2], (L, L), L ** -0.5, 1.0, (), jnp.float32),
        "slab_wts": jnp.clip(jnp.exp(jax.random.uniform(key_list[3], (SLABS, 4), jnp.float32, math.log(0.25), math.log(2.0))), 0.25, 2.0),
        "level_slab": draw_level_slab(jax.random.fold_in(key_list[5], 71), 0),
    }


dilation_steps = (1, 2, 4, 8)
highest = lax.Precision.HIGHEST

def line_filter(length, dilation):
    positions = jnp.arange(length)
    distance = jnp.abs(positions[None, :] - positions[:, None])
    inside = (distance % dilation == 0) & (distance <= 6 * dilation)
    ratio = (distance // dilation).astype(jnp.float32)
    kernel = jnp.where(inside, jnp.exp(-ratio * ratio / 8.0), 0.0).astype(jnp.float32)
    cubed = jnp.dot(jnp.dot(kernel, kernel, precision=highest), kernel, precision=highest)
    centre = cubed[:, length // 2]
    return cubed / jnp.sqrt(jnp.sum(centre * centre))

def horizontal(fields, weights, filters):
    running = jnp.zeros(fields.shape, jnp.float32)
    for scale_num in range(len(filters)):
        along_x, along_y = filters[scale_num]
        stepped = jnp.einsum('ij,...jy->...iy', along_x, fields, precision=highest)
        stepped = jnp.einsum('...iy,ly->...il', stepped, along_y, precision=highest)
        running = running + weights[:, scale_num][:, None, None] * stepped
    return running

def reference(control, ens_perts, vert_corr, slab_wts, level_slab):
    level_wts = slab_wts[level_slab]
    filters = [(line_filter(NX, dilation), line_filter(NY, dilation)) for dilation in dilation_steps]
    member_scale = 1.0 / math.sqrt(M - 1)

    def forward(level_field):
        smooth = horizontal(level_field, level_wts, filters)
        return jnp.einsum('lm,mxy->lxy', vert_corr, smooth, precision=highest)
    localized = lax.map(forward, control)
    wind_share = jnp.einsum('mclxy,mlxy->clxy', ens_perts, localized, precision=highest) * member_scale

    def backward(member_pert):
        adjoint = lax.optimization_barrier(jnp.sum(member_pert * wind_share, axis=0)) * member_scale
        adjoint = jnp.einsum('ml,mxy->lxy', vert_corr, adjoint, precision=highest)
        return horizontal(adjoint, level_wts, filters)
    gradient = control + lax.map(backward, ens_perts)
    return (wind_share, gradient)
```

```python
import functools
import math

import jax
import jax.numpy as jnp
import ml_dtypes
import numpy as np
from jax import lax
from jax.experimental import pallas as pl
from jax.experimental.pallas import tpu as pltpu
from jax.sharding import PartitionSpec as P

dilation_steps = (1, 2, 4, 8)
highest = lax.Precision.HIGHEST
MESH = pl.DeviceIdType.MESH
bf16 = jnp.bfloat16
f32 = jnp.float32
LANES = 128
SUB = 8


def line_filter(length, dilation):
    positions = np.arange(length)
    distance = np.abs(positions[None, :] - positions[:, None])
    inside = (distance % dilation == 0) & (distance <= 6 * dilation)
    ratio = (distance // dilation).astype(np.float64)
    kernel = np.where(inside, np.exp(-ratio * ratio / 8.0), 0.0)
    cubed = kernel @ kernel @ kernel
    centre = cubed[:, length // 2]
    return cubed / np.sqrt(np.sum(centre * centre))


def two_parts(matrix):
    high = matrix.astype(ml_dtypes.bfloat16)
    low = (matrix - high.astype(np.float64)).astype(ml_dtypes.bfloat16)
    return high, low


def x_matrices(tiles, rows, rows_pad):
    place = (np.arange(tiles)[:, None] * rows_pad + np.arange(rows)[None, :]).reshape(-1)
    found = []
    for dilation in dilation_steps:
        full = np.zeros((tiles * rows_pad,) * 2)
        full[np.ix_(place, place)] = line_filter(tiles * rows, dilation)
        high, low = two_parts(full)
        found.append(np.concatenate([high, high, low], axis=1))
    return np.stack(found)


def y_matrices(cols, slots, rest):
    result = []
    for slot in range(slots):
        place = np.concatenate([np.arange(LANES), LANES + slot * rest + np.arange(rest)])
        stacked = []
        for dilation in dilation_steps:
            full = np.zeros((2 * LANES, 2 * LANES))
            full[np.ix_(place, place)] = line_filter(cols, dilation).T
            stacked.append(full)
        result.append(np.stack(two_parts(np.concatenate(stacked, axis=0))))
    return np.stack(result)


def selectors(levels, tiles, slots):
    one = np.eye(levels, dtype=np.float32)
    main = np.repeat(one, SUB, axis=0)
    tile_num = np.arange(tiles)
    outer = np.stack([np.repeat(one[slots * tile_num + j], SUB, axis=0) for j in range(slots)])
    inner = np.stack([
        np.concatenate([
            np.repeat(one[slots * tile_num + (j - r) % slots], SUB, axis=0) for r in range(slots)
        ])
        for j in range(slots)
    ])
    return main, outer, inner


def kernel(
    dims,
    control_ref, pert_hbm, vert_ref, wl_ref, gx_hbm, by_hbm, main_sel, outer_sel, inner_sel,
    wind_ref, grad_ref,
    pert_raw, gx, by, send_a, f_a, y_a, s_a, pert, wp, cr, ws, xr, wf, send_b, f_b, y_b,
    fs, xh, xl, mix_main, mix_rest, back_main, back_rest,
    load_sem, a1s, a1r, a2s, a2r, a3s, a3r, a4s, a4r, c1s, c1r, xs, xrs, c2s, c2r,
):
    nt, nm, members, comps, levels, rows, rows_pad, cols, slots, rest, scale, order = dims
    planes = slots + 1
    scales = len(dilation_steps)
    all_x = nt * rows_pad
    nx = nm // 2
    nh = nt // 2
    chunks = rows_pad // SUB
    s_b = f_a
    me = lax.axis_index("tile")
    mem = lax.axis_index("mem")
    chip, core = mem // 2, lax.rem(mem, 2)
    partner = chip * 2 + (1 - core)

    loads = [
        pltpu.make_async_copy(pert_hbm.at[0], pert_raw, load_sem.at[0]),
        pltpu.make_async_copy(gx_hbm, gx, load_sem.at[1]),
        pltpu.make_async_copy(by_hbm, by, load_sem.at[2]),
    ]
    for load in loads:
        load.start()

    def packed(block):
        parts = [block[i, :, LANES:cols] for i in range(slots)]
        if rest * slots < LANES:
            parts.append(jnp.zeros((rows, LANES - rest * slots), f32))
        return jnp.concatenate(parts, axis=-1)

    def pack_to(block, out):
        if rows_pad != rows:
            out[...] = jnp.zeros((planes, rows_pad, LANES), f32)
        out[0:slots, 0:rows, :] = block[:, :, 0:LANES]
        out[slots, 0:rows, :] = packed(block)

    def tile_rank(k):
        return lax.rem(me + k, nt)

    barrier = pltpu.get_barrier_semaphore()
    for k in range(1, nt):
        pl.semaphore_signal(barrier, inc=1, device_id={"tile": tile_rank(k)}, device_id_type=MESH)
    pl.semaphore_signal(barrier, inc=1, device_id={"mem": partner}, device_id_type=MESH)
    for k in range(1, nx):
        other = lax.rem(chip + k, nx) * 2 + core
        pl.semaphore_signal(barrier, inc=1, device_id={"mem": other}, device_id_type=MESH)

    def pack_control(m):
        def body(t, carry):
            pack_to(control_ref[m, pl.ds(slots * t, slots)], send_a.at[m, t])
            return carry
        lax.fori_loop(0, nt, body, 0)

    pack_control(0)
    pl.semaphore_wait(barrier, (nt - 1) + 1 + (nx - 1))

    def exchange(src, dst, m, row, size, send_sem, recv_sem):
        span = pl.ds(row, size)
        for k in order:
            d = tile_rank(k)
            pltpu.make_async_remote_copy(
                src_ref=src.at[m, d, :, span, :], dst_ref=dst.at[m, me, :, span, :],
                send_sem=send_sem, recv_sem=recv_sem, device_id={"tile": d}, device_id_type=MESH,
            ).start()
        pltpu.make_async_copy(
            src.at[m, me, :, span, :], dst.at[m, me, :, span, :], recv_sem
        ).start()

    def arrived(dst, m, row, size, recv_sem):
        there = dst.at[m, :, :, pl.ds(row, size), :]
        pltpu.make_async_copy(there, there, recv_sem).wait()

    def sent(src, m, row, size, send_sem):
        there = src.at[m, pl.ds(0, nt - 1), :, pl.ds(row, size), :]
        pltpu.make_async_copy(there, there, send_sem).wait()

    exchange(send_a, f_a, 0, 0, rows_pad, a1s.at[0], a1r.at[0])
    for m in range(1, members):
        pack_control(m)
        exchange(send_a, f_a, m, 0, rows_pad, a1s.at[m], a1r.at[m])

    vert = vert_ref[...]
    same_row = lambda a, b: (
        lax.rem(lax.broadcasted_iota(jnp.int32, (a, b), 0), SUB)
        == lax.rem(lax.broadcasted_iota(jnp.int32, (a, b), 1), SUB)
    )

    def spread(left, right, flip):
        dot = functools.partial(lax.dot_general, precision=highest, preferred_element_type=f32)
        first = dot(left, vert, (((1,), (1 if flip else 0,)), ((), ())))
        wide = dot(first, right, (((1,), (1,)), ((), ())))
        return jnp.where(same_row(*wide.shape), wide, 0.0)

    for flip, main_out, rest_out in ((False, mix_main, mix_rest), (True, back_main, back_rest)):
        main_out[...] = spread(main_sel[...], main_sel[...], flip)
        for j in range(slots):
            rest_out[pl.ds(j * nt * SUB, nt * SUB), :] = spread(outer_sel[j], inner_sel[j], flip)

    for m in range(members):
        load = pltpu.make_async_copy(pert_hbm.at[m], pert_raw, load_sem.at[0])
        if m > 0:
            load.start()
        load.wait()

        def pack_pert(n, carry):
            c, t = n // nt, lax.rem(n, nt)
            pack_to(pert_raw[c, pl.ds(slots * t, slots)], pert.at[m, c, t])
            return carry
        lax.fori_loop(0, comps * nt, pack_pert, 0)
    loads[1].wait()
    loads[2].wait()

    def smooth(src, m, out):
        wide = jnp.concatenate(
            [src[m, :, p].reshape(all_x, LANES) for p in range(planes)], axis=1
        )
        high = wide.astype(bf16)
        low = (wide - high.astype(f32)).astype(bf16)
        fs[0:all_x, :] = high
        fs[all_x:2 * all_x, :] = low
        fs[2 * all_x:3 * all_x, :] = high

        def along_x(s, carry):
            stepped = jnp.dot(gx[s], fs[...], preferred_element_type=f32) * wl_ref[pl.ds(s, 1), :]
            up = stepped.astype(bf16)
            down = (stepped - up.astype(f32)).astype(bf16)
            for p in range(planes):
                xh[s, p] = up[:, p * LANES:(p + 1) * LANES]
                xl[s, p] = down[:, p * LANES:(p + 1) * LANES]
            return carry
        lax.fori_loop(0, scales, along_x, 0)

        def along_y(i, carry):
            pick = lambda ref: jnp.concatenate(
                [ref[s, p] for s in range(scales) for p in (i, slots)], axis=1
            )
            up, down = pick(xh), pick(xl)
            got = jnp.dot(up, by[i, 0], preferred_element_type=f32)
            got = got + jnp.dot(down, by[i, 0], preferred_element_type=f32)
            got = got + jnp.dot(up, by[i, 1], preferred_element_type=f32)
            got = got.reshape(nt, rows_pad, 2 * LANES)
            out[m, :, i] = got[:, :, 0:LANES]
            return carry + got[:, :, LANES:]
        rest_sum = lax.fori_loop(0, slots, along_y, jnp.zeros((nt, rows_pad, LANES), f32))
        out[m, :, slots] = rest_sum

    lane_group = lax.broadcasted_iota(jnp.int32, (nt * SUB, members * LANES), 1) % LANES // rest

    def mix(main_in, rest_in, main_mat, rest_mat):
        main_out = jnp.dot(main_mat[...], jnp.concatenate(main_in, axis=1),
                           precision=highest, preferred_element_type=f32)
        rolled = jnp.concatenate([
            jnp.concatenate(
                [x if r == 0 else pltpu.roll(x, r * rest, 1) for r in range(slots)], axis=0)
            for x in rest_in
        ], axis=1)
        rest_all = jnp.dot(rest_mat[...], rolled, precision=highest, preferred_element_type=f32)
        rest_out = jnp.zeros((nt * SUB, members * LANES), f32)
        for j in range(slots):
            rest_out = jnp.where(
                lane_group == j, rest_all[j * nt * SUB:(j + 1) * nt * SUB], rest_out)
        mains = [main_out[:, m * LANES:(m + 1) * LANES].reshape(nt, slots, SUB, LANES)
                 for m in range(members)]
        rests = [rest_out[:, m * LANES:(m + 1) * LANES].reshape(nt, SUB, LANES)
                 for m in range(members)]
        return mains, rests

    def span_of(c):
        return pl.ds(c * SUB, SUB)

    def core_copy(c, which):
        span = span_of(c)
        if which == 1:
            src, dst = wp.at[:, pl.ds((1 - core) * nh, nh), :, span, :], cr.at[:, :, :, span, :]
            sems = c1s.at[c], c1r.at[c]
        else:
            own = wf.at[:, pl.ds(core * nh, nh), :, span, :]
            src, dst, sems = own, own, (c2s.at[c], c2r.at[c])
        return pltpu.make_async_remote_copy(
            src_ref=src, dst_ref=dst, send_sem=sems[0], recv_sem=sems[1],
            device_id={"mem": partner}, device_id_type=MESH)

    def chip_copy(c, k):
        span = span_of(c)
        other = lax.rem(chip + k, nx) * 2 + core
        return pltpu.make_async_remote_copy(
            src_ref=ws.at[:, :, :, span, :], dst_ref=xr.at[k - 1, :, :, :, span, :],
            send_sem=xs.at[c, k - 1], recv_sem=xrs.at[c, k - 1],
            device_id={"mem": other}, device_id_type=MESH)

    def stage_mix(c):
        span = span_of(c)
        for m in range(members):
            arrived(s_a, m, c * SUB, SUB, a2r.at[m, c])
        mains, rests = mix(
            [s_a[m, :, 0:slots, span, :].reshape(levels * SUB, LANES) for m in range(members)],
            [s_a[m, :, slots, span, :].reshape(nt * SUB, LANES) for m in range(members)],
            mix_main, mix_rest)
        for comp in range(comps):
            main = pert[0, comp, :, 0:slots, span, :] * mains[0]
            tail = pert[0, comp, :, slots, span, :] * rests[0]
            for m in range(1, members):
                main = main + pert[m, comp, :, 0:slots, span, :] * mains[m]
                tail = tail + pert[m, comp, :, slots, span, :] * rests[m]
            wp[comp, :, 0:slots, span, :] = main
            wp[comp, :, slots, span, :] = tail
        core_copy(c, 1).start()

    def stage_chip(c):
        span = span_of(c)
        core_copy(c, 1).wait_recv()
        ws[:, :, :, span, :] = wp[:, pl.ds(core * nh, nh), :, span, :] + cr[:, :, :, span, :]
        for k in range(1, nx):
            chip_copy(c, k).start()

    def stage_full(c):
        span = span_of(c)
        total = ws[:, :, :, span, :]
        for k in range(1, nx):
            chip_copy(c, k).wait_recv()
            total = total + xr[k - 1, :, :, :, span, :]
        wf[:, pl.ds(core * nh, nh), :, span, :] = total * scale
        core_copy(c, 2).start()

    def stage_back(c):
        span = span_of(c)
        other_half = wf.at[:, pl.ds((1 - core) * nh, nh), :, span, :]
        pltpu.make_async_copy(other_half, other_half, c2r.at[c]).wait()
        mains, rests = [], []
        for m in range(members):
            main = pert[m, 0, :, 0:slots, span, :] * wf[0, :, 0:slots, span, :]
            tail = pert[m, 0, :, slots, span, :] * wf[0, :, slots, span, :]
            for comp in range(1, comps):
                main = main + pert[m, comp, :, 0:slots, span, :] * wf[comp, :, 0:slots, span, :]
                tail = tail + pert[m, comp, :, slots, span, :] * wf[comp, :, slots, span, :]
            mains.append((main * scale).reshape(levels * SUB, LANES))
            rests.append((tail * scale).reshape(nt * SUB, LANES))
        mains, rests = mix(mains, rests, back_main, back_rest)
        for m in range(members):
            send_b[m, :, 0:slots, span, :] = mains[m]
            send_b[m, :, slots, span, :] = rests[m]
            exchange(send_b, f_b, m, c * SUB, SUB, a3s.at[m, c], a3r.at[m, c])

    early = min(2, chunks)
    give_back = lambda m, c: exchange(y_a, s_a, m, c * SUB, SUB, a2s.at[m, c], a2r.at[m, c])
    for m in range(members):
        arrived(f_a, m, 0, rows_pad, a1r.at[m])
        smooth(f_a, m, y_a)
        for c in range(early):
            give_back(m, c)
    for c in range(early, chunks):
        for m in range(members):
            give_back(m, c)

    for step in range(chunks + 3):
        if 0 <= step - 3 < chunks:
            stage_back(step - 3)
        if 0 <= step - 2 < chunks:
            stage_full(step - 2)
        if 0 <= step - 1 < chunks:
            stage_chip(step - 1)
        if step < chunks:
            stage_mix(step)

    share = wind_ref.shape[1] // slots
    for comp in range(comps):
        for t in range(share):
            for i in range(slots):
                got = wf.at[comp, mem * share + t]
                wind_ref[comp, t * slots + i, :, 0:LANES] = got[i, 0:rows, :]
                wind_ref[comp, t * slots + i, :, LANES:cols] = got[slots, 0:rows, i * rest:(i + 1) * rest]

    for m in range(members):
        for c in range(chunks):
            arrived(f_b, m, c * SUB, SUB, a3r.at[m, c])
        smooth(f_b, m, y_b)
        exchange(y_b, s_b, m, 0, rows_pad, a4s.at[m], a4r.at[m])

    for m in range(members):
        arrived(s_b, m, 0, rows_pad, a4r.at[m])

        def finish(t, carry):
            for i in range(slots):
                lev = slots * t + i
                grad_ref[m, lev, :, 0:LANES] = (
                    control_ref[m, lev, :, 0:LANES] + s_b[m, t, i, 0:rows, :])
                grad_ref[m, lev, :, LANES:cols] = (
                    control_ref[m, lev, :, LANES:cols]
                    + s_b[m, t, slots, 0:rows, i * rest:(i + 1) * rest])
            return carry
        lax.fori_loop(0, nt, finish, 0)

    for m in range(members):
        sent(send_a, m, 0, rows_pad, a1s.at[m])
        sent(y_b, m, 0, rows_pad, a4s.at[m])
        for c in range(chunks):
            sent(y_a, m, c * SUB, SUB, a2s.at[m, c])
            sent(send_b, m, c * SUB, SUB, a3s.at[m, c])
    for c in range(chunks):
        core_copy(c, 1).wait_send()
        core_copy(c, 2).wait_send()
        for k in range(1, nx):
            chip_copy(c, k).wait_send()


def shards(mesh, control, ens_perts, vert_corr, slab_wts, level_slab):
    members, levels, rows, cols = control.shape
    comps = ens_perts.shape[1]
    nt, nm = mesh.shape["tile"], mesh.shape["mem"]
    slots = levels // nt
    planes = slots + 1
    rest = cols - LANES
    rows_pad = -(-rows // SUB) * SUB
    all_x = nt * rows_pad
    chunks = rows_pad // SUB
    nx, nh = nm // 2, nt // 2
    scale = 1.0 / math.sqrt(members * nm - 1)
    scales = len(dilation_steps)

    choose = (level_slab[:, None] == jnp.arange(slab_wts.shape[0])[None, :]).astype(f32)
    mine = lax.dynamic_slice_in_dim(choose, lax.axis_index("tile") * slots, slots, 0)
    mine = jnp.sum(mine[:, :, None] * slab_wts[None], axis=1)
    main_w = jnp.broadcast_to(mine.T[:, :, None], (scales, slots, LANES)).reshape(scales, -1)
    rest_w = jnp.broadcast_to(mine.T[:, :, None], (scales, slots, rest)).reshape(scales, -1)
    rest_w = jnp.pad(rest_w, ((0, 0), (0, LANES - rest * slots)))
    lane_wts = jnp.concatenate([main_w, rest_w], axis=1)

    gx = jnp.asarray(x_matrices(nt, rows, rows_pad))
    by = jnp.asarray(y_matrices(cols, slots, rest))
    picks = [jnp.asarray(a) for a in selectors(levels, nt, slots)]
    order = tuple(sorted(range(1, nt), key=lambda k: (abs(k - nt / 2), k)))
    dims = (nt, nm, members, comps, levels, rows, rows_pad, cols, slots, rest, scale, order)

    vmem = pl.BlockSpec(memory_space=pltpu.VMEM)
    anyspace = pl.BlockSpec(memory_space=pl.ANY)
    fields = pltpu.VMEM((members, nt, planes, rows_pad, LANES), f32)
    halfway = (comps, nh, planes, rows_pad, LANES)
    whole_wind = pltpu.VMEM((comps, nt, planes, rows_pad, LANES), f32)
    square = pltpu.VMEM((levels * SUB, levels * SUB), f32)
    dma = pltpu.SemaphoreType.DMA
    return pl.pallas_call(
        functools.partial(kernel, dims),
        out_shape=(
            jax.ShapeDtypeStruct((comps, levels // nm, rows, cols), f32),
            jax.ShapeDtypeStruct(control.shape, f32),
        ),
        in_specs=[vmem, anyspace, vmem, vmem, anyspace, anyspace, vmem, vmem, vmem],
        out_specs=(vmem, vmem),
        scratch_shapes=[
            pltpu.VMEM(ens_perts.shape[1:], f32),
            pltpu.VMEM(gx.shape, bf16),
            pltpu.VMEM(by.shape, bf16),
            fields, fields, fields, fields,
            pltpu.VMEM((members, comps, nt, planes, rows_pad, LANES), f32),
            whole_wind,
            pltpu.VMEM(halfway, f32),
            pltpu.VMEM(halfway, f32),
            pltpu.VMEM((nx - 1,) + halfway, f32),
            whole_wind,
            fields, fields, fields,
            pltpu.VMEM((3 * all_x, planes * LANES), bf16),
            pltpu.VMEM((scales, planes, all_x, LANES), bf16),
            pltpu.VMEM((scales, planes, all_x, LANES), bf16),
            square, square, square, square,
            dma((3,)),
            dma((members,)), dma((members,)),
            dma((members, chunks)), dma((members, chunks)),
            dma((members, chunks)), dma((members, chunks)),
            dma((members,)), dma((members,)),
            dma((chunks,)), dma((chunks,)),
            dma((chunks, nx - 1)), dma((chunks, nx - 1)),
            dma((chunks,)), dma((chunks,)),
        ],
        compiler_params=pltpu.CompilerParams(
            collective_id=0, has_side_effects=True, vmem_limit_bytes=58 * 2 ** 20),
        cost_estimate=pl.CostEstimate(
            flops=12 * 10 ** 9, bytes_accessed=30 * 10 ** 6, transcendentals=0),
    )(control, ens_perts, vert_corr, lane_wts, gx, by, *picks)


def solution(mesh):
    return jax.shard_map(
        functools.partial(shards, mesh),
        mesh=mesh,
        in_specs=(P("mem", None, "tile", None), P("mem", None, None, "tile", None), P(), P(), P()),
        out_specs=(P(None, "mem", "tile", None), P("mem", None, "tile", None)),
        check_vma=False,
    )
```

```python
import functools
import math

import jax
import jax.numpy as jnp
import ml_dtypes
import numpy as np
from jax import lax
from jax.experimental import pallas as pl
from jax.experimental.pallas import tpu as pltpu
from jax.sharding import PartitionSpec as P

dilation_steps = (1, 2, 4, 8)
highest = lax.Precision.HIGHEST
MESH = pl.DeviceIdType.MESH
bf16 = jnp.bfloat16
f32 = jnp.float32
LANES = 128
SUB = 8


def line_filter(length, dilation):
    positions = np.arange(length)
    distance = np.abs(positions[None, :] - positions[:, None])
    inside = (distance % dilation == 0) & (distance <= 6 * dilation)
    ratio = (distance // dilation).astype(np.float64)
    kernel = np.where(inside, np.exp(-ratio * ratio / 8.0), 0.0)
    cubed = kernel @ kernel @ kernel
    centre = cubed[:, length // 2]
    return cubed / np.sqrt(np.sum(centre * centre))


def two_parts(matrix):
    high = matrix.astype(ml_dtypes.bfloat16)
    low = (matrix - high.astype(np.float64)).astype(ml_dtypes.bfloat16)
    return high, low


def x_matrices(tiles, rows, rows_pad):
    place = (np.arange(tiles)[:, None] * rows_pad + np.arange(rows)[None, :]).reshape(-1)
    found = []
    for dilation in dilation_steps:
        full = np.zeros((tiles * rows_pad,) * 2)
        full[np.ix_(place, place)] = line_filter(tiles * rows, dilation)
        high, low = two_parts(full)
        found.append(np.concatenate([high, high, low], axis=1))
    return np.stack(found)


def y_matrices(cols, slots, rest):
    result = []
    for slot in range(slots):
        place = np.concatenate([np.arange(LANES), LANES + slot * rest + np.arange(rest)])
        stacked = []
        for dilation in dilation_steps:
            full = np.zeros((2 * LANES, 2 * LANES))
            full[np.ix_(place, place)] = line_filter(cols, dilation).T
            stacked.append(full)
        result.append(np.stack(two_parts(np.concatenate(stacked, axis=0))))
    return np.stack(result)


def selectors(levels, tiles, slots):
    one = np.eye(levels, dtype=np.float32)
    main = np.repeat(one, SUB, axis=0)
    tile_num = np.arange(tiles)
    outer = np.stack([np.repeat(one[slots * tile_num + j], SUB, axis=0) for j in range(slots)])
    inner = np.stack([
        np.concatenate([
            np.repeat(one[slots * tile_num + (j - r) % slots], SUB, axis=0) for r in range(slots)
        ])
        for j in range(slots)
    ])
    return main, outer, inner


def kernel(
    dims,
    control_ref, pert_hbm, vert_ref, slab_ref, level_ref, gx_hbm, by_hbm, main_sel, outer_sel, inner_sel,
    wind_ref, back_ref,
    pert_raw, gx, by, send_a, f_a, y_a, s_a, pert, wp, cr, ws, xr, wf, send_b, f_b, y_b,
    fs, xh, xl, wl_ref, mix_main, mix_rest, back_main, back_rest,
    load_sem, a1s, a1r, a2s, a2r, a3s, a3r, a4s, a4r, c1s, c1r, xs, xrs, c2s, c2r,
):
    nt, nm, members, comps, levels, rows, rows_pad, cols, slots, rest, scale, order = dims
    planes = slots + 1
    scales = len(dilation_steps)
    all_x = nt * rows_pad
    nx = nm // 2
    nh = nt // 2
    chunks = rows_pad // SUB
    s_b = f_a
    me = lax.axis_index("tile")
    mem = lax.axis_index("mem")
    chip, core = mem // 2, lax.rem(mem, 2)
    partner = chip * 2 + (1 - core)

    loads = [
        pltpu.make_async_copy(pert_hbm.at[0], pert_raw, load_sem.at[0]),
        pltpu.make_async_copy(gx_hbm, gx, load_sem.at[1]),
        pltpu.make_async_copy(by_hbm, by, load_sem.at[2]),
    ]
    for load in loads:
        load.start()

    def packed(block):
        parts = [block[i, :, LANES:cols] for i in range(slots)]
        if rest * slots < LANES:
            parts.append(jnp.zeros((rows, LANES - rest * slots), f32))
        return jnp.concatenate(parts, axis=-1)

    def pack_to(block, out):
        if rows_pad != rows:
            out[...] = jnp.zeros((planes, rows_pad, LANES), f32)
        out[0:slots, 0:rows, :] = block[:, :, 0:LANES]
        out[slots, 0:rows, :] = packed(block)

    def tile_rank(k):
        return lax.rem(me + k, nt)

    barrier = pltpu.get_barrier_semaphore()
    for k in range(1, nt):
        pl.semaphore_signal(barrier, inc=1, device_id={"tile": tile_rank(k)}, device_id_type=MESH)
    pl.semaphore_signal(barrier, inc=1, device_id={"mem": partner}, device_id_type=MESH)
    for k in range(1, nx):
        other = lax.rem(chip + k, nx) * 2 + core
        pl.semaphore_signal(barrier, inc=1, device_id={"mem": other}, device_id_type=MESH)

    def pack_control(m):
        def body(t, carry):
            pack_to(control_ref[m, pl.ds(slots * t, slots)], send_a.at[m, t])
            return carry
        lax.fori_loop(0, nt, body, 0)

    pack_control(0)
    pl.semaphore_wait(barrier, (nt - 1) + 1 + (nx - 1))

    def exchange(src, dst, m, row, size, send_sem, recv_sem):
        span = pl.ds(row, size)
        for k in order:
            d = tile_rank(k)
            pltpu.make_async_remote_copy(
                src_ref=src.at[m, d, :, span, :], dst_ref=dst.at[m, me, :, span, :],
                send_sem=send_sem, recv_sem=recv_sem, device_id={"tile": d}, device_id_type=MESH,
            ).start()
        pltpu.make_async_copy(
            src.at[m, me, :, span, :], dst.at[m, me, :, span, :], recv_sem
        ).start()

    def arrived(dst, m, row, size, recv_sem):
        there = dst.at[m, :, :, pl.ds(row, size), :]
        pltpu.make_async_copy(there, there, recv_sem).wait()

    def sent(src, m, row, size, send_sem):
        there = src.at[m, pl.ds(0, nt - 1), :, pl.ds(row, size), :]
        pltpu.make_async_copy(there, there, send_sem).wait()

    exchange(send_a, f_a, 0, 0, rows_pad, a1s.at[0], a1r.at[0])
    for m in range(1, members):
        pack_control(m)
        exchange(send_a, f_a, m, 0, rows_pad, a1s.at[m], a1r.at[m])

    vert = vert_ref[...]
    slabs = slab_ref.shape[0]
    column = lambda a, b: lax.dot_general(
        a, b, (((0,), (0,)), ((), ())), precision=highest, preferred_element_type=f32)
    choose = (
        lax.broadcasted_iota(jnp.int32, (slabs, levels), 0) == level_ref[...]).astype(f32)
    lane = lax.broadcasted_iota(jnp.int32, (levels, planes * LANES), 1)
    lane_slot = jnp.where(lane < slots * LANES, lane // LANES, (lane - slots * LANES) // rest)
    own = (lax.broadcasted_iota(jnp.int32, lane.shape, 0) == me * slots + lane_slot).astype(f32)
    wl_ref[...] = column(column(choose, slab_ref[...]), own)
    same_row = lambda a, b: (
        lax.rem(lax.broadcasted_iota(jnp.int32, (a, b), 0), SUB)
        == lax.rem(lax.broadcasted_iota(jnp.int32, (a, b), 1), SUB)
    )

    def spread(left, right, flip):
        dot = functools.partial(lax.dot_general, precision=highest, preferred_element_type=f32)
        first = dot(left, vert, (((1,), (1 if flip else 0,)), ((), ())))
        wide = dot(first, right, (((1,), (1,)), ((), ())))
        return jnp.where(same_row(*wide.shape), wide, 0.0)

    for flip, main_out, rest_out in ((False, mix_main, mix_rest), (True, back_main, back_rest)):
        main_out[...] = spread(main_sel[...], main_sel[...], flip)
        for j in range(slots):
            rest_out[pl.ds(j * nt * SUB, nt * SUB), :] = spread(outer_sel[j], inner_sel[j], flip)

    for m in range(members):
        load = pltpu.make_async_copy(pert_hbm.at[m], pert_raw, load_sem.at[0])
        if m > 0:
            load.start()
        load.wait()

        def pack_pert(n, carry):
            c, t = n // nt, lax.rem(n, nt)
            pack_to(pert_raw[c, pl.ds(slots * t, slots)], pert.at[m, c, t])
            return carry
        lax.fori_loop(0, comps * nt, pack_pert, 0)
    loads[1].wait()
    loads[2].wait()

    def smooth(src, m, out):
        wide = jnp.concatenate(
            [src[m, :, p].reshape(all_x, LANES) for p in range(planes)], axis=1
        )
        high = wide.astype(bf16)
        low = (wide - high.astype(f32)).astype(bf16)
        fs[0:all_x, :] = high
        fs[all_x:2 * all_x, :] = low
        fs[2 * all_x:3 * all_x, :] = high

        def along_x(s, carry):
            stepped = jnp.dot(gx[s], fs[...], preferred_element_type=f32) * wl_ref[pl.ds(s, 1), :]
            up = stepped.astype(bf16)
            down = (stepped - up.astype(f32)).astype(bf16)
            for p in range(planes):
                xh[s, p] = up[:, p * LANES:(p + 1) * LANES]
                xl[s, p] = down[:, p * LANES:(p + 1) * LANES]
            return carry
        lax.fori_loop(0, scales, along_x, 0)

        def along_y(i, carry):
            pick = lambda ref: jnp.concatenate(
                [ref[s, p] for s in range(scales) for p in (i, slots)], axis=1
            )
            up, down = pick(xh), pick(xl)
            got = jnp.dot(up, by[i, 0], preferred_element_type=f32)
            got = got + jnp.dot(down, by[i, 0], preferred_element_type=f32)
            got = got + jnp.dot(up, by[i, 1], preferred_element_type=f32)
            got = got.reshape(nt, rows_pad, 2 * LANES)
            out[m, :, i] = got[:, :, 0:LANES]
            return carry + got[:, :, LANES:]
        rest_sum = lax.fori_loop(0, slots, along_y, jnp.zeros((nt, rows_pad, LANES), f32))
        out[m, :, slots] = rest_sum

    lane_group = lax.broadcasted_iota(jnp.int32, (nt * SUB, members * LANES), 1) % LANES // rest

    def mix(main_in, rest_in, main_mat, rest_mat):
        main_out = jnp.dot(main_mat[...], jnp.concatenate(main_in, axis=1),
                           precision=highest, preferred_element_type=f32)
        rolled = jnp.concatenate([
            jnp.concatenate(
                [x if r == 0 else pltpu.roll(x, r * rest, 1) for r in range(slots)], axis=0)
            for x in rest_in
        ], axis=1)
        rest_all = jnp.dot(rest_mat[...], rolled, precision=highest, preferred_element_type=f32)
        rest_out = jnp.zeros((nt * SUB, members * LANES), f32)
        for j in range(slots):
            rest_out = jnp.where(
                lane_group == j, rest_all[j * nt * SUB:(j + 1) * nt * SUB], rest_out)
        mains = [main_out[:, m * LANES:(m + 1) * LANES].reshape(nt, slots, SUB, LANES)
                 for m in range(members)]
        rests = [rest_out[:, m * LANES:(m + 1) * LANES].reshape(nt, SUB, LANES)
                 for m in range(members)]
        return mains, rests

    def span_of(c):
        return pl.ds(c * SUB, SUB)

    def core_copy(c, which):
        span = span_of(c)
        if which == 1:
            src, dst = wp.at[:, pl.ds((1 - core) * nh, nh), :, span, :], cr.at[:, :, :, span, :]
            sems = c1s.at[c], c1r.at[c]
        else:
            own = wf.at[:, pl.ds(core * nh, nh), :, span, :]
            src, dst, sems = own, own, (c2s.at[c], c2r.at[c])
        return pltpu.make_async_remote_copy(
            src_ref=src, dst_ref=dst, send_sem=sems[0], recv_sem=sems[1],
            device_id={"mem": partner}, device_id_type=MESH)

    def chip_copy(c, k):
        span = span_of(c)
        other = lax.rem(chip + k, nx) * 2 + core
        return pltpu.make_async_remote_copy(
            src_ref=ws.at[:, :, :, span, :], dst_ref=xr.at[k - 1, :, :, :, span, :],
            send_sem=xs.at[c, k - 1], recv_sem=xrs.at[c, k - 1],
            device_id={"mem": other}, device_id_type=MESH)

    def stage_mix(c):
        span = span_of(c)
        for m in range(members):
            arrived(s_a, m, c * SUB, SUB, a2r.at[m, c])
        mains, rests = mix(
            [s_a[m, :, 0:slots, span, :].reshape(levels * SUB, LANES) for m in range(members)],
            [s_a[m, :, slots, span, :].reshape(nt * SUB, LANES) for m in range(members)],
            mix_main, mix_rest)
        for comp in range(comps):
            main = pert[0, comp, :, 0:slots, span, :] * mains[0]
            tail = pert[0, comp, :, slots, span, :] * rests[0]
            for m in range(1, members):
                main = main + pert[m, comp, :, 0:slots, span, :] * mains[m]
                tail = tail + pert[m, comp, :, slots, span, :] * rests[m]
            wp[comp, :, 0:slots, span, :] = main
            wp[comp, :, slots, span, :] = tail
        core_copy(c, 1).start()

    def stage_chip(c):
        span = span_of(c)
        core_copy(c, 1).wait_recv()
        ws[:, :, :, span, :] = wp[:, pl.ds(core * nh, nh), :, span, :] + cr[:, :, :, span, :]
        for k in range(1, nx):
            chip_copy(c, k).start()

    def stage_full(c):
        span = span_of(c)
        total = ws[:, :, :, span, :]
        for k in range(1, nx):
            chip_copy(c, k).wait_recv()
            total = total + xr[k - 1, :, :, :, span, :]
        wf[:, pl.ds(core * nh, nh), :, span, :] = total * scale
        core_copy(c, 2).start()

    early = min(2, chunks)
    send_adjoint = lambda m, c: exchange(
        send_b, f_b, m, c * SUB, SUB, a3s.at[m, c], a3r.at[m, c])

    def stage_back(c):
        span = span_of(c)
        other_half = wf.at[:, pl.ds((1 - core) * nh, nh), :, span, :]
        pltpu.make_async_copy(other_half, other_half, c2r.at[c]).wait()
        mains, rests = [], []
        for m in range(members):
            main = pert[m, 0, :, 0:slots, span, :] * wf[0, :, 0:slots, span, :]
            tail = pert[m, 0, :, slots, span, :] * wf[0, :, slots, span, :]
            for comp in range(1, comps):
                main = main + pert[m, comp, :, 0:slots, span, :] * wf[comp, :, 0:slots, span, :]
                tail = tail + pert[m, comp, :, slots, span, :] * wf[comp, :, slots, span, :]
            mains.append((main * scale).reshape(levels * SUB, LANES))
            rests.append((tail * scale).reshape(nt * SUB, LANES))
        mains, rests = mix(mains, rests, back_main, back_rest)
        for m in range(members):
            send_b[m, :, 0:slots, span, :] = mains[m]
            send_b[m, :, slots, span, :] = rests[m]
            if m == 0 or c < early:
                send_adjoint(m, c)

    give_back = lambda m, c: exchange(y_a, s_a, m, c * SUB, SUB, a2s.at[m, c], a2r.at[m, c])
    for m in range(members):
        arrived(f_a, m, 0, rows_pad, a1r.at[m])
        smooth(f_a, m, y_a)
        for c in range(early):
            give_back(m, c)
    for c in range(early, chunks):
        for m in range(members):
            give_back(m, c)

    for step in range(chunks + 3):
        if 0 <= step - 3 < chunks:
            stage_back(step - 3)
        if 0 <= step - 2 < chunks:
            stage_full(step - 2)
        if 0 <= step - 1 < chunks:
            stage_chip(step - 1)
        if step < chunks:
            stage_mix(step)

    for m in range(1, members):
        for c in range(early, chunks):
            send_adjoint(m, c)

    share = wind_ref.shape[1]
    wind_ref[...] = wf[:, pl.ds(mem * share, share)]

    for m in range(members):
        for c in range(chunks):
            arrived(f_b, m, c * SUB, SUB, a3r.at[m, c])
        smooth(f_b, m, y_b)
        exchange(y_b, s_b, m, 0, rows_pad, a4s.at[m], a4r.at[m])

    for m in range(members):
        arrived(s_b, m, 0, rows_pad, a4r.at[m])
        back_ref[m] = s_b[m]

    for m in range(members):
        sent(send_a, m, 0, rows_pad, a1s.at[m])
        sent(y_b, m, 0, rows_pad, a4s.at[m])
        for c in range(chunks):
            sent(y_a, m, c * SUB, SUB, a2s.at[m, c])
            sent(send_b, m, c * SUB, SUB, a3s.at[m, c])
    for c in range(chunks):
        core_copy(c, 1).wait_send()
        core_copy(c, 2).wait_send()
        for k in range(1, nx):
            chip_copy(c, k).wait_send()


def unpack_kernel(rest, control_ref, back_ref, wind_packed, grad_ref, wind_ref):
    rows, cols = control_ref.shape[-2:]
    slots = back_ref.shape[2] - 1

    def level(tiles, t, i):
        return (tiles[0, t, i, 0:rows, :], tiles[0, t, slots, 0:rows, i * rest:(i + 1) * rest])

    for t in range(back_ref.shape[1]):
        for i in range(slots):
            lev = slots * t + i
            main, tail = level(back_ref, t, i)
            grad_ref[0, lev, :, 0:LANES] = control_ref[0, lev, :, 0:LANES] + main
            grad_ref[0, lev, :, LANES:cols] = control_ref[0, lev, :, LANES:cols] + tail

    @pl.when(pl.program_id(0) == 0)
    def _():
        for comp in range(wind_packed.shape[0]):
            for t in range(wind_packed.shape[1]):
                for i in range(slots):
                    main, tail = level(wind_packed.at[pl.ds(comp, 1)], t, i)
                    wind_ref[comp, slots * t + i, :, 0:LANES] = main
                    wind_ref[comp, slots * t + i, :, LANES:cols] = tail


def shards(mesh, control, ens_perts, vert_corr, slab_wts, level_slab):
    members, levels, rows, cols = control.shape
    comps = ens_perts.shape[1]
    nt, nm = mesh.shape["tile"], mesh.shape["mem"]
    slots = levels // nt
    planes = slots + 1
    rest = cols - LANES
    rows_pad = -(-rows // SUB) * SUB
    all_x = nt * rows_pad
    chunks = rows_pad // SUB
    nx, nh = nm // 2, nt // 2
    scale = 1.0 / math.sqrt(members * nm - 1)
    scales = len(dilation_steps)

    gx = jnp.asarray(x_matrices(nt, rows, rows_pad))
    by = jnp.asarray(y_matrices(cols, slots, rest))
    picks = [jnp.asarray(a) for a in selectors(levels, nt, slots)]
    order = tuple(sorted(range(1, nt), key=lambda k: (abs(k - nt / 2), k)))
    dims = (nt, nm, members, comps, levels, rows, rows_pad, cols, slots, rest, scale, order)

    vmem = pl.BlockSpec(memory_space=pltpu.VMEM)
    anyspace = pl.BlockSpec(memory_space=pl.ANY)
    fields = pltpu.VMEM((members, nt, planes, rows_pad, LANES), f32)
    halfway = (comps, nh, planes, rows_pad, LANES)
    whole_wind = pltpu.VMEM((comps, nt, planes, rows_pad, LANES), f32)
    square = pltpu.VMEM((levels * SUB, levels * SUB), f32)
    dma = pltpu.SemaphoreType.DMA
    share = levels // nm // slots
    wind_packed, back_packed = pl.pallas_call(
        functools.partial(kernel, dims),
        out_shape=(
            jax.ShapeDtypeStruct((comps, share, planes, rows_pad, LANES), f32),
            jax.ShapeDtypeStruct((members, nt, planes, rows_pad, LANES), f32),
        ),
        in_specs=[vmem, anyspace, vmem, vmem, vmem, anyspace, anyspace, vmem, vmem, vmem],
        out_specs=(vmem, vmem),
        scratch_shapes=[
            pltpu.VMEM(ens_perts.shape[1:], f32),
            pltpu.VMEM(gx.shape, bf16),
            pltpu.VMEM(by.shape, bf16),
            fields, fields, fields, fields,
            pltpu.VMEM((members, comps, nt, planes, rows_pad, LANES), f32),
            whole_wind,
            pltpu.VMEM(halfway, f32),
            pltpu.VMEM(halfway, f32),
            pltpu.VMEM((nx - 1,) + halfway, f32),
            whole_wind,
            fields, fields, fields,
            pltpu.VMEM((3 * all_x, planes * LANES), bf16),
            pltpu.VMEM((scales, planes, all_x, LANES), bf16),
            pltpu.VMEM((scales, planes, all_x, LANES), bf16),
            pltpu.VMEM((scales, planes * LANES), f32),
            square, square, square, square,
            dma((3,)),
            dma((members,)), dma((members,)),
            dma((members, chunks)), dma((members, chunks)),
            dma((members, chunks)), dma((members, chunks)),
            dma((members,)), dma((members,)),
            dma((chunks,)), dma((chunks,)),
            dma((chunks, nx - 1)), dma((chunks, nx - 1)),
            dma((chunks,)), dma((chunks,)),
        ],
        compiler_params=pltpu.CompilerParams(
            collective_id=0, has_side_effects=True, vmem_limit_bytes=58 * 2 ** 20),
        cost_estimate=pl.CostEstimate(
            flops=12 * 10 ** 9, bytes_accessed=30 * 10 ** 6, transcendentals=0),
    )(control, ens_perts, vert_corr, slab_wts, level_slab.reshape(1, levels), gx, by, *picks)

    halves = 2
    by_half = lambda n: (n // halves, n % halves, 0, 0)
    all_wind = pl.BlockSpec(wind_packed.shape, lambda n: (0, 0, 0, 0, 0))
    field_block = pl.BlockSpec((1, levels // halves, rows, cols), by_half)
    wind_shape = (comps, levels // nm, rows, cols)
    gradient, wind_share = pl.pallas_call(
        functools.partial(unpack_kernel, rest),
        grid=(members * halves,),
        out_shape=(
            jax.ShapeDtypeStruct(control.shape, f32), jax.ShapeDtypeStruct(wind_shape, f32)),
        in_specs=[
            field_block,
            pl.BlockSpec((1, nt // halves, planes, rows_pad, LANES), lambda n: by_half(n) + (0,)),
            all_wind,
        ],
        out_specs=(field_block, pl.BlockSpec(wind_shape, lambda n: (0, 0, 0, 0))),
        compiler_params=pltpu.CompilerParams(vmem_limit_bytes=58 * 2 ** 20),
        cost_estimate=pl.CostEstimate(
            flops=2 * 10 ** 6, bytes_accessed=8 * 10 ** 6, transcendentals=0),
    )(control, back_packed, wind_packed)
    return wind_share, gradient


def solution(mesh):
    return jax.shard_map(
        functools.partial(shards, mesh),
        mesh=mesh,
        in_specs=(P("mem", None, "tile", None), P("mem", None, None, "tile", None), P(), P(), P()),
        out_specs=(P(None, "mem", "tile", None), P("mem", None, "tile", None)),
        check_vma=False,
    )
```

```python
import functools
import math

import jax
import jax.numpy as jnp
import ml_dtypes
import numpy as np
from jax import lax
from jax.experimental import pallas as pl
from jax.experimental.pallas import tpu as pltpu
from jax.sharding import PartitionSpec as P

dilation_steps = (1, 2, 4, 8)
highest = lax.Precision.HIGHEST
MESH = pl.DeviceIdType.MESH
bf16 = jnp.bfloat16
f32 = jnp.float32
LANES = 128
SUB = 8


def line_filter(length, dilation):
    positions = np.arange(length)
    distance = np.abs(positions[None, :] - positions[:, None])
    inside = (distance % dilation == 0) & (distance <= 6 * dilation)
    ratio = (distance // dilation).astype(np.float64)
    kernel = np.where(inside, np.exp(-ratio * ratio / 8.0), 0.0)
    cubed = kernel @ kernel @ kernel
    centre = cubed[:, length // 2]
    return cubed / np.sqrt(np.sum(centre * centre))


def two_parts(matrix):
    high = matrix.astype(ml_dtypes.bfloat16)
    low = (matrix - high.astype(np.float64)).astype(ml_dtypes.bfloat16)
    return high, low


def x_matrices(tiles, rows, rows_pad):
    place = (np.arange(tiles)[:, None] * rows_pad + np.arange(rows)[None, :]).reshape(-1)
    found = []
    for dilation in dilation_steps:
        full = np.zeros((tiles * rows_pad,) * 2)
        full[np.ix_(place, place)] = line_filter(tiles * rows, dilation)
        high, low = two_parts(full)
        found.append(np.concatenate([high, high, low], axis=1))
    return np.stack(found)


def y_matrices(cols, slots, rest):
    result = []
    for slot in range(slots):
        place = np.concatenate([np.arange(LANES), LANES + slot * rest + np.arange(rest)])
        stacked = []
        for dilation in dilation_steps:
            full = np.zeros((2 * LANES, 2 * LANES))
            full[np.ix_(place, place)] = line_filter(cols, dilation).T
            stacked.append(full)
        result.append(np.stack(two_parts(np.concatenate(stacked, axis=0))))
    return np.stack(result)


def selectors(levels, tiles, slots):
    one = np.eye(levels, dtype=np.float32)
    main = np.repeat(one, SUB, axis=0)
    tile_num = np.arange(tiles)
    outer = np.stack([np.repeat(one[slots * tile_num + j], SUB, axis=0) for j in range(slots)])
    inner = np.stack([
        np.concatenate([
            np.repeat(one[slots * tile_num + (j - r) % slots], SUB, axis=0) for r in range(slots)
        ])
        for j in range(slots)
    ])
    return main, outer, inner


def kernel(
    dims,
    control_hbm, pert_hbm, vert_ref, slab_ref, level_ref, gx_hbm, by_hbm, main_sel, outer_sel, inner_sel,
    wind_hbm, back_hbm,
    control_ref, pert_raw, gx, by, send_a, f_a, y_a, s_a, pert, wp, cr, ws, xr, wf, send_b, f_b, y_b,
    fs, xh, xl, wl_ref, mix_main, mix_rest, back_main, back_rest,
    load_sem, field_sem, out_sem, a1s, a1r, a2s, a2r, a3s, a3r, a4s, a4r, c1s, c1r, xs, xrs, c2s, c2r,
):
    nt, nm, members, comps, levels, rows, rows_pad, cols, slots, rest, scale, order = dims
    planes = slots + 1
    scales = len(dilation_steps)
    all_x = nt * rows_pad
    nx = nm // 2
    nh = nt // 2
    chunks = rows_pad // SUB
    s_b = f_a
    me = lax.axis_index("tile")
    mem = lax.axis_index("mem")
    chip, core = mem // 2, lax.rem(mem, 2)
    partner = chip * 2 + (1 - core)

    loads = [
        pltpu.make_async_copy(pert_hbm.at[0], pert_raw, load_sem.at[0]),
        pltpu.make_async_copy(gx_hbm, gx, load_sem.at[1]),
        pltpu.make_async_copy(by_hbm, by, load_sem.at[2]),
    ]
    fields_in = [
        pltpu.make_async_copy(control_hbm.at[m], control_ref.at[m], field_sem.at[m])
        for m in range(members)
    ]
    for load in fields_in + loads:
        load.start()

    def packed(block):
        parts = [block[i, :, LANES:cols] for i in range(slots)]
        if rest * slots < LANES:
            parts.append(jnp.zeros((rows, LANES - rest * slots), f32))
        return jnp.concatenate(parts, axis=-1)

    def pack_to(block, out):
        if rows_pad != rows:
            out[...] = jnp.zeros((planes, rows_pad, LANES), f32)
        out[0:slots, 0:rows, :] = block[:, :, 0:LANES]
        out[slots, 0:rows, :] = packed(block)

    def tile_rank(k):
        return lax.rem(me + k, nt)

    barrier = pltpu.get_barrier_semaphore()
    for k in range(1, nt):
        pl.semaphore_signal(barrier, inc=1, device_id={"tile": tile_rank(k)}, device_id_type=MESH)
    pl.semaphore_signal(barrier, inc=1, device_id={"mem": partner}, device_id_type=MESH)
    for k in range(1, nx):
        other = lax.rem(chip + k, nx) * 2 + core
        pl.semaphore_signal(barrier, inc=1, device_id={"mem": other}, device_id_type=MESH)

    def pack_control(m):
        fields_in[m].wait()

        def body(t, carry):
            pack_to(control_ref[m, pl.ds(slots * t, slots)], send_a.at[m, t])
            return carry
        lax.fori_loop(0, nt, body, 0)

    pack_control(0)
    pl.semaphore_wait(barrier, (nt - 1) + 1 + (nx - 1))

    def exchange(src, dst, m, row, size, send_sem, recv_sem):
        span = pl.ds(row, size)
        for k in order:
            d = tile_rank(k)
            pltpu.make_async_remote_copy(
                src_ref=src.at[m, d, :, span, :], dst_ref=dst.at[m, me, :, span, :],
                send_sem=send_sem, recv_sem=recv_sem, device_id={"tile": d}, device_id_type=MESH,
            ).start()
        pltpu.make_async_copy(
            src.at[m, me, :, span, :], dst.at[m, me, :, span, :], recv_sem
        ).start()

    def arrived(dst, m, row, size, recv_sem):
        there = dst.at[m, :, :, pl.ds(row, size), :]
        pltpu.make_async_copy(there, there, recv_sem).wait()

    def sent(src, m, row, size, send_sem):
        there = src.at[m, pl.ds(0, nt - 1), :, pl.ds(row, size), :]
        pltpu.make_async_copy(there, there, send_sem).wait()

    exchange(send_a, f_a, 0, 0, rows_pad, a1s.at[0], a1r.at[0])
    for m in range(1, members):
        pack_control(m)
        exchange(send_a, f_a, m, 0, rows_pad, a1s.at[m], a1r.at[m])

    vert = vert_ref[...]
    slabs = slab_ref.shape[1]
    exact = functools.partial(jnp.dot, precision=highest, preferred_element_type=f32)
    choose = (
        lax.broadcasted_iota(jnp.int32, (slabs, levels), 0) == level_ref[...]).astype(f32)
    lane = lax.broadcasted_iota(jnp.int32, (levels, planes * LANES), 1)
    lane_slot = jnp.where(lane < slots * LANES, lane // LANES, (lane - slots * LANES) // rest)
    own = (lax.broadcasted_iota(jnp.int32, lane.shape, 0) == me * slots + lane_slot).astype(f32)
    wl_ref[...] = exact(exact(slab_ref[...], choose), own)
    same_row = lambda a, b: (
        lax.rem(lax.broadcasted_iota(jnp.int32, (a, b), 0), SUB)
        == lax.rem(lax.broadcasted_iota(jnp.int32, (a, b), 1), SUB)
    )

    def spread(left, right, flip):
        dot = functools.partial(lax.dot_general, precision=highest, preferred_element_type=f32)
        first = dot(left, vert, (((1,), (1 if flip else 0,)), ((), ())))
        wide = dot(first, right, (((1,), (1,)), ((), ())))
        return jnp.where(same_row(*wide.shape), wide, 0.0)

    for flip, main_out, rest_out in ((False, mix_main, mix_rest), (True, back_main, back_rest)):
        main_out[...] = spread(main_sel[...], main_sel[...], flip)
        for j in range(slots):
            rest_out[pl.ds(j * nt * SUB, nt * SUB), :] = spread(outer_sel[j], inner_sel[j], flip)

    for m in range(members):
        load = pltpu.make_async_copy(pert_hbm.at[m], pert_raw, load_sem.at[0])
        if m > 0:
            load.start()
        load.wait()

        def pack_pert(n, carry):
            c, t = n // nt, lax.rem(n, nt)
            pack_to(pert_raw[c, pl.ds(slots * t, slots)], pert.at[m, c, t])
            return carry
        lax.fori_loop(0, comps * nt, pack_pert, 0)
    loads[1].wait()
    loads[2].wait()

    def smooth(src, m, out):
        wide = jnp.concatenate(
            [src[m, :, p].reshape(all_x, LANES) for p in range(planes)], axis=1
        )
        high = wide.astype(bf16)
        low = (wide - high.astype(f32)).astype(bf16)
        fs[0:all_x, :] = high
        fs[all_x:2 * all_x, :] = low
        fs[2 * all_x:3 * all_x, :] = high

        def along_x(s, carry):
            stepped = jnp.dot(gx[s], fs[...], preferred_element_type=f32) * wl_ref[pl.ds(s, 1), :]
            up = stepped.astype(bf16)
            down = (stepped - up.astype(f32)).astype(bf16)
            for p in range(planes):
                xh[s, p] = up[:, p * LANES:(p + 1) * LANES]
                xl[s, p] = down[:, p * LANES:(p + 1) * LANES]
            return carry
        lax.fori_loop(0, scales, along_x, 0)

        def along_y(i, carry):
            pick = lambda ref: jnp.concatenate(
                [ref[s, p] for s in range(scales) for p in (i, slots)], axis=1
            )
            up, down = pick(xh), pick(xl)
            got = jnp.dot(up, by[i, 0], preferred_element_type=f32)
            got = got + jnp.dot(down, by[i, 0], preferred_element_type=f32)
            got = got + jnp.dot(up, by[i, 1], preferred_element_type=f32)
            got = got.reshape(nt, rows_pad, 2 * LANES)
            out[m, :, i] = got[:, :, 0:LANES]
            return carry + got[:, :, LANES:]
        rest_sum = lax.fori_loop(0, slots, along_y, jnp.zeros((nt, rows_pad, LANES), f32))
        out[m, :, slots] = rest_sum

    lane_group = lax.broadcasted_iota(jnp.int32, (nt * SUB, members * LANES), 1) % LANES // rest

    def mix(main_in, rest_in, main_mat, rest_mat):
        main_out = jnp.dot(main_mat[...], jnp.concatenate(main_in, axis=1),
                           precision=highest, preferred_element_type=f32)
        rolled = jnp.concatenate([
            jnp.concatenate(
                [x if r == 0 else pltpu.roll(x, r * rest, 1) for r in range(slots)], axis=0)
            for x in rest_in
        ], axis=1)
        rest_all = jnp.dot(rest_mat[...], rolled, precision=highest, preferred_element_type=f32)
        rest_out = jnp.zeros((nt * SUB, members * LANES), f32)
        for j in range(slots):
            rest_out = jnp.where(
                lane_group == j, rest_all[j * nt * SUB:(j + 1) * nt * SUB], rest_out)
        mains = [main_out[:, m * LANES:(m + 1) * LANES].reshape(nt, slots, SUB, LANES)
                 for m in range(members)]
        rests = [rest_out[:, m * LANES:(m + 1) * LANES].reshape(nt, SUB, LANES)
                 for m in range(members)]
        return mains, rests

    def span_of(c):
        return pl.ds(c * SUB, SUB)

    def core_copy(c, which):
        span = span_of(c)
        if which == 1:
            src, dst = wp.at[:, pl.ds((1 - core) * nh, nh), :, span, :], cr.at[:, :, :, span, :]
            sems = c1s.at[c], c1r.at[c]
        else:
            own = wf.at[:, pl.ds(core * nh, nh), :, span, :]
            src, dst, sems = own, own, (c2s.at[c], c2r.at[c])
        return pltpu.make_async_remote_copy(
            src_ref=src, dst_ref=dst, send_sem=sems[0], recv_sem=sems[1],
            device_id={"mem": partner}, device_id_type=MESH)

    def chip_copy(c, k):
        span = span_of(c)
        other = lax.rem(chip + k, nx) * 2 + core
        return pltpu.make_async_remote_copy(
            src_ref=ws.at[:, :, :, span, :], dst_ref=xr.at[k - 1, :, :, :, span, :],
            send_sem=xs.at[c, k - 1], recv_sem=xrs.at[c, k - 1],
            device_id={"mem": other}, device_id_type=MESH)

    def stage_mix(c):
        span = span_of(c)
        for m in range(members):
            arrived(s_a, m, c * SUB, SUB, a2r.at[m, c])
        mains, rests = mix(
            [s_a[m, :, 0:slots, span, :].reshape(levels * SUB, LANES) for m in range(members)],
            [s_a[m, :, slots, span, :].reshape(nt * SUB, LANES) for m in range(members)],
            mix_main, mix_rest)
        for comp in range(comps):
            main = pert[0, comp, :, 0:slots, span, :] * mains[0]
            tail = pert[0, comp, :, slots, span, :] * rests[0]
            for m in range(1, members):
                main = main + pert[m, comp, :, 0:slots, span, :] * mains[m]
                tail = tail + pert[m, comp, :, slots, span, :] * rests[m]
            wp[comp, :, 0:slots, span, :] = main
            wp[comp, :, slots, span, :] = tail
        core_copy(c, 1).start()

    def stage_chip(c):
        span = span_of(c)
        core_copy(c, 1).wait_recv()
        ws[:, :, :, span, :] = wp[:, pl.ds(core * nh, nh), :, span, :] + cr[:, :, :, span, :]
        for k in range(1, nx):
            chip_copy(c, k).start()

    def stage_full(c):
        span = span_of(c)
        total = ws[:, :, :, span, :]
        for k in range(1, nx):
            chip_copy(c, k).wait_recv()
            total = total + xr[k - 1, :, :, :, span, :]
        wf[:, pl.ds(core * nh, nh), :, span, :] = total * scale
        core_copy(c, 2).start()

    early = min(2, chunks)
    send_adjoint = lambda m, c: exchange(
        send_b, f_b, m, c * SUB, SUB, a3s.at[m, c], a3r.at[m, c])

    def stage_back(c):
        span = span_of(c)
        other_half = wf.at[:, pl.ds((1 - core) * nh, nh), :, span, :]
        pltpu.make_async_copy(other_half, other_half, c2r.at[c]).wait()
        mains, rests = [], []
        for m in range(members):
            main = pert[m, 0, :, 0:slots, span, :] * wf[0, :, 0:slots, span, :]
            tail = pert[m, 0, :, slots, span, :] * wf[0, :, slots, span, :]
            for comp in range(1, comps):
                main = main + pert[m, comp, :, 0:slots, span, :] * wf[comp, :, 0:slots, span, :]
                tail = tail + pert[m, comp, :, slots, span, :] * wf[comp, :, slots, span, :]
            mains.append((main * scale).reshape(levels * SUB, LANES))
            rests.append((tail * scale).reshape(nt * SUB, LANES))
        mains, rests = mix(mains, rests, back_main, back_rest)
        for m in range(members):
            send_b[m, :, 0:slots, span, :] = mains[m]
            send_b[m, :, slots, span, :] = rests[m]
            if m == 0 or c < early:
                send_adjoint(m, c)

    ahead = min(3, chunks)
    give_back = lambda m, c: exchange(y_a, s_a, m, c * SUB, SUB, a2s.at[m, c], a2r.at[m, c])
    for m in range(members):
        arrived(f_a, m, 0, rows_pad, a1r.at[m])
        smooth(f_a, m, y_a)
        for c in range(ahead):
            give_back(m, c)
    for c in range(ahead, chunks):
        for m in range(members):
            give_back(m, c)

    for step in range(chunks + 3):
        if 0 <= step - 3 < chunks:
            stage_back(step - 3)
        if 0 <= step - 2 < chunks:
            stage_full(step - 2)
        if 0 <= step - 1 < chunks:
            stage_chip(step - 1)
        if step < chunks:
            stage_mix(step)

    for m in range(1, members):
        for c in range(early, chunks):
            send_adjoint(m, c)

    share = wind_hbm.shape[1]
    results = [pltpu.make_async_copy(
        wf.at[:, pl.ds(mem * share, share)], wind_hbm, out_sem.at[members])]
    results[0].start()

    for m in range(members):
        for c in range(chunks):
            arrived(f_b, m, c * SUB, SUB, a3r.at[m, c])
        smooth(f_b, m, y_b)
        exchange(y_b, s_b, m, 0, rows_pad, a4s.at[m], a4r.at[m])

    for m in range(members):
        arrived(s_b, m, 0, rows_pad, a4r.at[m])
        results.append(pltpu.make_async_copy(s_b.at[m], back_hbm.at[m], out_sem.at[m]))
        results[-1].start()

    for result in results:
        result.wait()
    for m in range(members):
        sent(send_a, m, 0, rows_pad, a1s.at[m])
        sent(y_b, m, 0, rows_pad, a4s.at[m])
        for c in range(chunks):
            sent(y_a, m, c * SUB, SUB, a2s.at[m, c])
            sent(send_b, m, c * SUB, SUB, a3s.at[m, c])
    for c in range(chunks):
        core_copy(c, 1).wait_send()
        core_copy(c, 2).wait_send()
        for k in range(1, nx):
            chip_copy(c, k).wait_send()


def unpack_kernel(rest, control_ref, back_ref, wind_packed, grad_ref, wind_ref):
    rows, cols = control_ref.shape[-2:]
    slots = back_ref.shape[2] - 1

    def level(tiles, t, i):
        return (tiles[0, t, i, 0:rows, :], tiles[0, t, slots, 0:rows, i * rest:(i + 1) * rest])

    for t in range(back_ref.shape[1]):
        for i in range(slots):
            lev = slots * t + i
            main, tail = level(back_ref, t, i)
            grad_ref[0, lev, :, 0:LANES] = control_ref[0, lev, :, 0:LANES] + main
            grad_ref[0, lev, :, LANES:cols] = control_ref[0, lev, :, LANES:cols] + tail

    @pl.when(pl.program_id(0) == 0)
    def _():
        for comp in range(wind_packed.shape[0]):
            for t in range(wind_packed.shape[1]):
                for i in range(slots):
                    main, tail = level(wind_packed.at[pl.ds(comp, 1)], t, i)
                    wind_ref[comp, slots * t + i, :, 0:LANES] = main
                    wind_ref[comp, slots * t + i, :, LANES:cols] = tail


def shards(mesh, control, ens_perts, vert_corr, slab_wts, level_slab):
    members, levels, rows, cols = control.shape
    comps = ens_perts.shape[1]
    nt, nm = mesh.shape["tile"], mesh.shape["mem"]
    slots = levels // nt
    planes = slots + 1
    rest = cols - LANES
    rows_pad = -(-rows // SUB) * SUB
    all_x = nt * rows_pad
    chunks = rows_pad // SUB
    nx, nh = nm // 2, nt // 2
    scale = 1.0 / math.sqrt(members * nm - 1)
    scales = len(dilation_steps)

    gx = jnp.asarray(x_matrices(nt, rows, rows_pad))
    by = jnp.asarray(y_matrices(cols, slots, rest))
    picks = [jnp.asarray(a) for a in selectors(levels, nt, slots)]
    order = tuple(sorted(range(1, nt), key=lambda k: (abs(k - nt / 2), k)))
    dims = (nt, nm, members, comps, levels, rows, rows_pad, cols, slots, rest, scale, order)

    vmem = pl.BlockSpec(memory_space=pltpu.VMEM)
    anyspace = pl.BlockSpec(memory_space=pl.ANY)
    fields = pltpu.VMEM((members, nt, planes, rows_pad, LANES), f32)
    halfway = (comps, nh, planes, rows_pad, LANES)
    whole_wind = pltpu.VMEM((comps, nt, planes, rows_pad, LANES), f32)
    square = pltpu.VMEM((levels * SUB, levels * SUB), f32)
    dma = pltpu.SemaphoreType.DMA
    share = levels // nm // slots
    wind_packed, back_packed = pl.pallas_call(
        functools.partial(kernel, dims),
        out_shape=(
            jax.ShapeDtypeStruct((comps, share, planes, rows_pad, LANES), f32),
            jax.ShapeDtypeStruct((members, nt, planes, rows_pad, LANES), f32),
        ),
        in_specs=[anyspace, anyspace, vmem, vmem, vmem, anyspace, anyspace, vmem, vmem, vmem],
        out_specs=(anyspace, anyspace),
        scratch_shapes=[
            pltpu.VMEM(control.shape, f32),
            pltpu.VMEM(ens_perts.shape[1:], f32),
            pltpu.VMEM(gx.shape, bf16),
            pltpu.VMEM(by.shape, bf16),
            fields, fields, fields, fields,
            pltpu.VMEM((members, comps, nt, planes, rows_pad, LANES), f32),
            whole_wind,
            pltpu.VMEM(halfway, f32),
            pltpu.VMEM(halfway, f32),
            pltpu.VMEM((nx - 1,) + halfway, f32),
            whole_wind,
            fields, fields, fields,
            pltpu.VMEM((3 * all_x, planes * LANES), bf16),
            pltpu.VMEM((scales, planes, all_x, LANES), bf16),
            pltpu.VMEM((scales, planes, all_x, LANES), bf16),
            pltpu.VMEM((scales, planes * LANES), f32),
            square, square, square, square,
            dma((3,)), dma((members,)), dma((members + 1,)),
            dma((members,)), dma((members,)),
            dma((members, chunks)), dma((members, chunks)),
            dma((members, chunks)), dma((members, chunks)),
            dma((members,)), dma((members,)),
            dma((chunks,)), dma((chunks,)),
            dma((chunks, nx - 1)), dma((chunks, nx - 1)),
            dma((chunks,)), dma((chunks,)),
        ],
        compiler_params=pltpu.CompilerParams(
            collective_id=0, has_side_effects=True, vmem_limit_bytes=58 * 2 ** 20),
        cost_estimate=pl.CostEstimate(
            flops=12 * 10 ** 9, bytes_accessed=30 * 10 ** 6, transcendentals=0),
    )(control, ens_perts, vert_corr, slab_wts.T, level_slab.reshape(1, levels), gx, by, *picks)

    halves = 2
    by_half = lambda n: (n // halves, n % halves, 0, 0)
    all_wind = pl.BlockSpec(wind_packed.shape, lambda n: (0, 0, 0, 0, 0))
    field_block = pl.BlockSpec((1, levels // halves, rows, cols), by_half)
    wind_shape = (comps, levels // nm, rows, cols)
    gradient, wind_share = pl.pallas_call(
        functools.partial(unpack_kernel, rest),
        grid=(members * halves,),
        out_shape=(
            jax.ShapeDtypeStruct(control.shape, f32), jax.ShapeDtypeStruct(wind_shape, f32)),
        in_specs=[
            field_block,
            pl.BlockSpec((1, nt // halves, planes, rows_pad, LANES), lambda n: by_half(n) + (0,)),
            all_wind,
        ],
        out_specs=(field_block, pl.BlockSpec(wind_shape, lambda n: (0, 0, 0, 0))),
        compiler_params=pltpu.CompilerParams(vmem_limit_bytes=58 * 2 ** 20),
        cost_estimate=pl.CostEstimate(
            flops=2 * 10 ** 6, bytes_accessed=8 * 10 ** 6, transcendentals=0),
    )(control, back_packed, wind_packed)
    return wind_share, gradient


def solution(mesh):
    return jax.shard_map(
        functools.partial(shards, mesh),
        mesh=mesh,
        in_specs=(P("mem", None, "tile", None), P("mem", None, None, "tile", None), P(), P(), P()),
        out_specs=(P(None, "mem", "tile", None), P("mem", None, "tile", None)),
        check_vma=False,
    )
```
